256 devices in a mesh: bx: 16 (over z, core), by: 16 (over x, y).
Axes of the slice: x: 4, y: 4, z: 8, core: 2. Of those that a mesh axis runs over, the one named last changes fastest.
Arguments:
- density: bfloat16 [16, 16, 16, 64, 4096], P('bx', 'by'), may hold values from -5 to 5
- inner_order: int32 [16], replicated, may hold values from 0 to 15, each once
- outer_order: int32 [16], replicated, may hold values from 0 to 15, each once
- footprints: int32 [16, 16, 4], P('bx', 'by'), may hold values from 0 to 4096, as said below
Outputs:
- composite: float32 [4, 64, 4096], P(None, None, 'bx')
The draws below stay inside these ranges and needn't reach their ends.
Inputs may be any that keep to these rules, and one draw needn't show every extreme that they name: footprints[i, j] holds first row, end row, first column and end column of brick (i, j)'s rectangle, first below end; rows lie in 0 to 64; one brick's rectangle is the whole band.
All inputs are finite; a program needn't handle non-finite values.
Results may differ from the reference program's by a relative error of at most 0.0005.
Values may be sent and summed in bfloat16 or wider, within the bound.
A program may use at most 128 MiB of HBM per device.

```python
import jax
import jax.numpy as jnp
from jax import lax

ROWS = 64
COLS = 4096
DEPTH = 16
XBRICKS = 16
YBRICKS = 16


def draw_footprints(key, part):
    key = jax.random.fold_in(key, 7)
    keys = jax.random.split(key, 5)
    shape = (XBRICKS, YBRICKS)
    margin = max(ROWS // 4, 1)
    half_cols = COLS // 2
    top_row = jax.random.randint(keys[0], shape, 0, margin)
    end_row = ROWS - jax.random.randint(keys[1], shape, 0, margin)
    left_col = jax.random.randint(keys[2], shape, 0, half_cols)
    end_col = COLS - jax.random.randint(keys[3], shape, 0, half_cols)
    picked = jax.random.randint(keys[4], (), 0, XBRICKS * YBRICKS)
    chosen = jnp.arange(XBRICKS * YBRICKS, dtype=jnp.int32).reshape(shape) == picked
    top_row = jnp.where(chosen, 0, top_row)
    end_row = jnp.where(chosen, ROWS, end_row)
    left_col = jnp.where(chosen, 0, left_col)
    end_col = jnp.where(chosen, COLS, end_col)
    return jnp.stack([top_row, end_row, left_col, end_col], axis=-1).astype(jnp.int32)


def block_levels(key, shape, cuts, least, largest):
    def one(axis_at, shards_of):
        draws = jax.random.uniform(jax.random.fold_in(jax.random.fold_in(key, 6), axis_at), (shards_of,), jnp.float32, least / len(cuts), largest / len(cuts))
        return jnp.repeat(jnp.exp(draws), shape[axis_at] // shards_of).reshape((-1,) + (1,) * (len(shape) - axis_at - 1))

    gain = one(*cuts[0])
    for cut in cuts[1:]:
        gain = gain * one(*cut)
    return gain


def bell_draw(stream_key, extent, spread, bound, cuts=(), kind=jnp.bfloat16):
    values = jax.random.normal(stream_key, extent, jnp.float32) * spread
    if len(cuts) > 0:
        values = block_levels(stream_key, extent, cuts, -0.22, 0.18) * values
    return jnp.clip(values, min=-bound, max=bound).astype(kind)


def setup_inputs(seed: int = 0) -> dict:
    seeds = jax.random.split(jax.random.key(seed), 5)
    density = bell_draw(seeds[0], (XBRICKS, YBRICKS, DEPTH, ROWS, COLS), 1.0, 5.0, ((0, 16), (1, 16)))
    inner_order = jax.random.permutation(seeds[1], XBRICKS).astype(jnp.int32)
    outer_order = jax.random.permutation(seeds[2], YBRICKS).astype(jnp.int32)
    footprints = draw_footprints(jax.random.fold_in(seeds[4], 71), 0)
    return {"density": density, "inner_order": inner_order, "outer_order": outer_order, "footprints": footprints}


def palette(values):
    return jnp.stack([jax.nn.sigmoid(2.0 * values), jnp.exp(-0.5 * values * values), jax.nn.sigmoid(-2.0 * values)], axis=0)


def render_slab(slab_data, extinct):
    colour = jnp.zeros((3,) + slab_data.shape[1:], jnp.float32)
    transmit = jnp.ones(slab_data.shape[1:], jnp.float32)
    for sample in range(slab_data.shape[0]):
        values = slab_data[sample].astype(jnp.float32)
        optical = extinct * values * values + 2.0 * jnp.maximum(values - 2.5, 0.0)
        survive = jnp.exp(-optical)
        colour = colour + (transmit * (1.0 - survive))[None] * palette(values)
        transmit = transmit * survive
    return jnp.concatenate([colour, (1.0 - transmit)[None]], axis=0)


def blend_over(front, behind):
    return front + (1.0 - front[3])[None] * behind


def invert_order(order):
    count = order.shape[0]
    ranks = jnp.arange(count, dtype=jnp.int32)
    return jnp.sum(ranks[:, None] * (order[:, None] == ranks[None, :]).astype(jnp.int32), axis=0).astype(jnp.int32)


def reference(density, inner_order, outer_order, footprints):
    extinct = 1.5 / (XBRICKS * YBRICKS * DEPTH)
    inner_inverse = invert_order(inner_order)
    outer_inverse = invert_order(outer_order)
    row_index = jnp.arange(ROWS, dtype=jnp.int32)[:, None]
    col_index = jnp.arange(COLS, dtype=jnp.int32)[None, :]

    def advance(blended, rank):
        first = inner_inverse[rank % XBRICKS]
        second = outer_inverse[rank // XBRICKS]
        slab_data = density[first, second]
        bounds = footprints[first, second]
        inside = (row_index >= bounds[0]) & (row_index < bounds[1]) & (col_index >= bounds[2]) & (col_index < bounds[3])
        masked = slab_data * inside.astype(jnp.bfloat16)[None]
        return blend_over(blended, render_slab(masked, extinct)), None

    start = jnp.zeros((4, ROWS, COLS), jnp.float32)
    composite, unused = lax.scan(advance, start, jnp.arange(XBRICKS * YBRICKS, dtype=jnp.int32))
    return composite
```

```python
import functools

import jax
import jax.numpy as jnp
from jax import lax
from jax.experimental import pallas as pl
from jax.experimental.pallas import tpu as pltpu
from jax.sharding import PartitionSpec as P

MESH = pl.DeviceIdType.MESH
LOG2E = 1.4426950408889634
TILE_ROWS = 16
WIDTH = 256
FIRST = 2
CODE = 65534.0


def encode(value):
    root = lax.rsqrt(lax.rsqrt(jnp.maximum(value, 0.0)))
    return (root * CODE + 0.5).astype(jnp.int32).astype(jnp.uint16)


def decode(code):
    root = code.astype(jnp.int32).astype(jnp.float32)
    square = root * root * (1.0 / (CODE * CODE))
    return square * square


def march(load, depth, extinct):
    transmit = tanhs = green = None
    for sample in range(depth):
        values = load(sample).astype(jnp.float32)
        square = values * values
        bend = jnp.minimum((2.5 - values) * (2.0 * LOG2E), 0.0)
        survive = jnp.exp2(square * (-extinct * LOG2E) + bend)
        bell = jnp.exp2(square * (-0.5 * LOG2E))
        slope = jnp.tanh(values)
        if sample == 0:
            left = survive
            weight = 1.0 - survive
            tanhs = weight * slope
            green = weight * bell
        else:
            left = transmit * survive
            weight = transmit - left
            tanhs = tanhs + weight * slope
            green = green + weight * bell
        transmit = left
    opaque = 1.0 - transmit
    return 0.5 * (opaque + tanhs), green, 0.5 * (opaque - tanhs)


def blend(images, order_ref, count):
    red = green = blue = through = None
    for rank in range(count):
        at = order_ref[rank]
        r, g, b = images[at, 0], images[at, 1], images[at, 2]
        clear = 1.0 - (r + b)
        if rank == 0:
            red, green, blue, through = r, g, b, clear
        else:
            red = red + through * r
            green = green + through * g
            blue = blue + through * b
            through = through * clear
    return red, green, blue


def kernel(
    sizes,
    extinct,
    inner_hbm,
    outer_hbm,
    bounds_hbm,
    density_ref,
    out_ref,
    slab,
    sending,
    landed,
    groups,
    images,
    inner_ref,
    outer_ref,
    bounds_ref,
    inner_inverse,
    outer_inverse,
    small_sem,
    load_sem,
    send_sem,
    recv_sem,
    group_send_sem,
    group_recv_sem,
):
    across_x, across_y, side, depth, rows, columns = sizes
    chips = across_x // 2
    block = columns // across_x
    halves = block // WIDTH
    pieces = rows // TILE_ROWS * halves
    strips = rows // TILE_ROWS
    i = lax.axis_index("bx")
    j = lax.axis_index("by")
    z, core = i // 2, i % 2
    x, y = j // side, j % side

    def column_peer(n):
        step = n // 2
        hops = chips // 2 + (1 - 2 * (step % 2)) * ((step + 1) // 2)
        return (z + hops) % chips * 2 + (core + 1 - n % 2) % 2

    def group_peer(n):
        return (x + n // side) % side * side + (y + n % side) % side

    def load(strip):
        return pltpu.make_async_copy(
            density_ref.at[0, 0, :, pl.ds(pl.multiple_of(strip * TILE_ROWS, TILE_ROWS), TILE_ROWS), :],
            slab.at[strip],
            load_sem.at[strip],
        )

    def column_copy(piece, n):
        return pltpu.make_async_remote_copy(
            src_ref=sending.at[piece, n],
            dst_ref=landed.at[piece, i],
            send_sem=send_sem.at[piece, n],
            recv_sem=recv_sem.at[piece, i],
            device_id=(column_peer(n), j),
            device_id_type=MESH,
        )

    def column_arrival(piece, n):
        peer = column_peer(n)
        return pltpu.make_async_remote_copy(
            src_ref=sending.at[piece, n],
            dst_ref=landed.at[piece, peer],
            send_sem=send_sem.at[piece, n],
            recv_sem=recv_sem.at[piece, peer],
            device_id=(peer, j),
            device_id_type=MESH,
        )

    def group_copy(piece, n):
        return pltpu.make_async_remote_copy(
            src_ref=groups.at[piece, j],
            dst_ref=groups.at[piece, j],
            send_sem=group_send_sem.at[piece, n],
            recv_sem=group_recv_sem.at[piece, j],
            device_id=(i, group_peer(n)),
            device_id_type=MESH,
        )

    def group_arrival(piece, n):
        peer = group_peer(n)
        return pltpu.make_async_remote_copy(
            src_ref=groups.at[piece, j],
            dst_ref=groups.at[piece, peer],
            send_sem=group_send_sem.at[piece, n],
            recv_sem=group_recv_sem.at[piece, peer],
            device_id=(i, peer),
            device_id_type=MESH,
        )

    def each(count, act, first=0):
        def step(n, carry):
            act(n)
            return carry

        lax.fori_loop(first, count, step, 0)

    def render(piece, n, store):
        strip = piece // halves
        left = pl.multiple_of(column_peer(n) * block + piece % halves * WIDTH, WIDTH)
        colours = march(lambda s: slab[strip, s, :, pl.ds(left, WIDTH)], depth, extinct)
        row = lax.broadcasted_iota(jnp.int32, (TILE_ROWS, WIDTH), 0) + strip * TILE_ROWS
        column = lax.broadcasted_iota(jnp.int32, (TILE_ROWS, WIDTH), 1) + left
        inside = (
            (row >= bounds_ref[0, 0, 0])
            & (row < bounds_ref[0, 0, 1])
            & (column >= bounds_ref[0, 0, 2])
            & (column < bounds_ref[0, 0, 3])
        )
        for channel, colour in enumerate(colours):
            store(channel, encode(jnp.where(inside, colour, 0.0)))

    def render_send(piece, n):
        def store(channel, codes):
            sending[piece, n, channel] = codes

        render(piece, n, store)

    def render_keep(piece):
        def keep(channel, codes):
            landed[piece, i, channel] = codes

        render(piece, across_x - 1, keep)

    def take(buffer, piece, at):
        codes = buffer[piece, at]
        for channel in range(3):
            images[at, channel] = decode(codes[channel])

    def finish(piece):
        take(groups, piece, j)

        def arrive(n):
            group_arrival(piece, n).wait_recv()
            take(groups, piece, group_peer(n))

        each(across_y, arrive, 1)
        red, green, blue = blend(images, outer_inverse, across_y)
        top = pl.multiple_of(piece // halves * TILE_ROWS, TILE_ROWS)
        left = pl.multiple_of(piece % halves * WIDTH, WIDTH)
        where = (pl.ds(top, TILE_ROWS), pl.ds(left, WIDTH))
        out_ref[(0,) + where] = red
        out_ref[(1,) + where] = green
        out_ref[(2,) + where] = blue
        out_ref[(3,) + where] = red + blue

    small = [
        pltpu.make_async_copy(inner_hbm, inner_ref, small_sem.at[0]),
        pltpu.make_async_copy(outer_hbm, outer_ref, small_sem.at[1]),
        pltpu.make_async_copy(bounds_hbm, bounds_ref, small_sem.at[2]),
    ]
    small[2].start()
    each(strips, lambda strip: load(strip).start())
    small[0].start()
    small[1].start()

    barrier = pltpu.get_barrier_semaphore()

    def greet_column(n):
        pl.semaphore_signal(barrier, inc=1, device_id=(column_peer(n), j), device_id_type=MESH)

    def greet_group(n):
        pl.semaphore_signal(barrier, inc=1, device_id=(i, group_peer(n)), device_id_type=MESH)

    each(across_x - 1, greet_column)
    each(across_y, greet_group, 1)

    small[2].wait()
    load(0).wait()
    each(FIRST, lambda n: render_send(0, n))
    pl.semaphore_wait(barrier, across_x - 1 + across_y - 1)
    each(FIRST, lambda n: column_copy(0, n).start())

    def render_and_send(piece, n):
        render_send(piece, n)
        column_copy(piece, n).start()

    each(across_x - 1, lambda n: render_and_send(0, n), FIRST)
    render_keep(0)

    def follow(piece):
        @pl.when(piece % halves == 0)
        def _():
            load(piece // halves).wait()

        each(across_x - 1, lambda n: render_and_send(piece, n))
        render_keep(piece)

    each(pieces, follow, 1)

    def invert(order_ref, inverse_ref, count):
        def one(rank):
            found = jnp.int32(0)
            for at in range(count):
                found = jnp.where(order_ref[at] == rank, at, found)
            inverse_ref[rank] = found

        each(count, one)

    small[0].wait()
    small[1].wait()
    invert(inner_ref, inner_inverse, across_x)
    invert(outer_ref, outer_inverse, across_y)

    def advance(piece):
        take(landed, piece, i)

        def arrive(n):
            column_arrival(piece, n).wait_recv()
            take(landed, piece, column_peer(n))

        each(across_x - 1, arrive)
        red, green, blue = blend(images, inner_inverse, across_x)
        groups[piece, j, 0] = encode(red)
        groups[piece, j, 1] = encode(green)
        groups[piece, j, 2] = encode(blue)
        each(across_y, lambda n: group_copy(piece, n).start(), 1)

        @pl.when(piece >= 1)
        def _():
            finish(piece - 1)

    each(pieces, advance)
    finish(pieces - 1)

    def drain(piece):
        each(across_x - 1, lambda n: column_copy(piece, n).wait_send())
        each(across_y, lambda n: group_copy(piece, n).wait_send(), 1)

    each(pieces, drain)


def on_device(density, inner_order, outer_order, footprints):
    across_x = lax.axis_size("bx")
    across_y = lax.axis_size("by")
    depth, rows, columns = density.shape[2:]
    extinct = 1.5 / (across_x * across_y * depth)
    side = 1
    while side * side < across_y:
        side *= 2
    block = columns // across_x
    pieces = rows // TILE_ROWS * (block // WIDTH)
    strips = rows // TILE_ROWS
    piece_shape = (3, TILE_ROWS, WIDTH)
    hbm = pl.BlockSpec(memory_space=pltpu.HBM)
    return pl.pallas_call(
        functools.partial(kernel, (across_x, across_y, side, depth, rows, columns), extinct),
        out_shape=jax.ShapeDtypeStruct((4, rows, block), jnp.float32),
        in_specs=[hbm] * 4,
        out_specs=pl.BlockSpec(memory_space=pltpu.VMEM),
        scratch_shapes=[
            pltpu.VMEM((strips, depth, TILE_ROWS, columns), jnp.bfloat16),
            pltpu.VMEM((pieces, across_x - 1) + piece_shape, jnp.uint16),
            pltpu.VMEM((pieces, across_x) + piece_shape, jnp.uint16),
            pltpu.VMEM((pieces, across_y) + piece_shape, jnp.uint16),
            pltpu.VMEM((max(across_x, across_y),) + piece_shape, jnp.float32),
            pltpu.SMEM((across_x,), jnp.int32),
            pltpu.SMEM((across_y,), jnp.int32),
            pltpu.SMEM((1, 1, 4), jnp.int32),
            pltpu.SMEM((across_x,), jnp.int32),
            pltpu.SMEM((across_y,), jnp.int32),
            pltpu.SemaphoreType.DMA((3,)),
            pltpu.SemaphoreType.DMA((strips,)),
            pltpu.SemaphoreType.DMA((pieces, across_x)),
            pltpu.SemaphoreType.DMA((pieces, across_x)),
            pltpu.SemaphoreType.DMA((pieces, across_y)),
            pltpu.SemaphoreType.DMA((pieces, across_y)),
        ],
        compiler_params=pltpu.CompilerParams(
            collective_id=0, has_side_effects=True, vmem_limit_bytes=60 << 20
        ),
    )(inner_order, outer_order, footprints, density)


def solution(mesh):
    in_specs = (P("bx", "by", None, None, None), P(), P(), P("bx", "by", None))
    out_specs = P(None, None, "bx")
    return jax.shard_map(
        on_device, mesh=mesh, in_specs=in_specs, out_specs=out_specs, check_vma=False
    )
```

```python
import functools

import jax
import jax.numpy as jnp
from jax import lax
from jax.experimental import pallas as pl
from jax.experimental.pallas import tpu as pltpu
from jax.sharding import PartitionSpec as P

MESH = pl.DeviceIdType.MESH
LOG2E = 1.4426950408889634
STRIP = 16
CUTS = 2
FIRST = 2
CODE = 65534.0


def encode(value):
    root = lax.rsqrt(lax.rsqrt(jnp.clip(value, 0.0, 1.0)))
    return (root * CODE + 0.5).astype(jnp.int32).astype(jnp.uint16)


def decode(code):
    root = code.astype(jnp.int32).astype(jnp.float32)
    square = root * root * (1.0 / (CODE * CODE))
    return square * square


def march(load, depth, extinct):
    transmit = tanhs = green = None
    for sample in range(depth):
        values = load(sample).astype(jnp.float32)
        square = values * values
        bend = jnp.minimum((2.5 - values) * (2.0 * LOG2E), 0.0)
        survive = jnp.exp2(square * (-extinct * LOG2E) + bend)
        bell = jnp.exp2(square * (-0.5 * LOG2E))
        slope = jnp.tanh(values)
        if sample == 0:
            left = survive
            weight = 1.0 - survive
            tanhs = weight * slope
            green = weight * bell
        else:
            left = transmit * survive
            weight = transmit - left
            tanhs = tanhs + weight * slope
            green = green + weight * bell
        transmit = left
    opaque = 1.0 - transmit
    return 0.5 * (opaque + tanhs), green, 0.5 * (opaque - tanhs)


def blend(images, order_ref, count, width):
    red = green = blue = through = None
    for rank in range(count):
        at = order_ref[rank]
        r, g, b = (images[at, channel, :, :width] for channel in range(3))
        clear = 1.0 - (r + b)
        if rank == 0:
            red, green, blue, through = r, g, b, clear
        else:
            red = red + through * r
            green = green + through * g
            blue = blue + through * b
            through = through * clear
    return red, green, blue


def kernel(
    sizes,
    extinct,
    inner_hbm,
    outer_hbm,
    bounds_hbm,
    density_ref,
    out_ref,
    result,
    slab,
    sending,
    landed,
    groups,
    images,
    inner_ref,
    outer_ref,
    bounds_ref,
    inner_inverse,
    outer_inverse,
    small_sem,
    load_sem,
    send_sem,
    recv_sem,
    group_send_sem,
    group_recv_sem,
    out_sem,
):
    across_x, across_y, side, depth, rows, columns = sizes
    chips = across_x // 2
    block = columns // across_x
    strips = rows // STRIP
    cut = block // CUTS
    last = strips - 1
    pieces = [(strip, 0, block) for strip in range(last)]
    pieces += [(last, cut * at, cut) for at in range(CUTS)]
    i = lax.axis_index("bx")
    j = lax.axis_index("by")
    z, core = i // 2, i % 2
    x, y = j // side, j % side

    def column_peer(n):
        step = n % chips
        hops = chips // 2 + (1 - 2 * (step % 2)) * ((step + 1) // 2)
        return (z + hops) % chips * 2 + (core + 1 - n // chips) % 2

    def group_peer(n):
        return (x + n // side) % side * side + (y + n % side) % side

    def load(strip):
        return pltpu.make_async_copy(
            density_ref.at[0, 0, :, pl.ds(pl.multiple_of(strip * STRIP, STRIP), STRIP), :],
            slab.at[strip],
            load_sem.at[strip],
        )

    def remote(src, dst, sends, recvs, device):
        return pltpu.make_async_remote_copy(
            src_ref=src, dst_ref=dst, send_sem=sends, recv_sem=recvs, device_id=device, device_id_type=MESH
        )

    def view(buffer, piece, at):
        strip, left, width = piece
        return buffer.at[strip, at, :, :, pl.ds(left, width)]

    def number(piece):
        strip, left, width = piece
        return strip + left // width

    def column_copy(piece, n, slot):
        return remote(
            view(sending, piece, n),
            view(landed, piece, slot),
            send_sem.at[number(piece), n],
            recv_sem.at[number(piece), slot],
            (column_peer(n), j),
        )

    def group_copy(piece, n, slot):
        return remote(
            view(groups, piece, j),
            view(groups, piece, slot),
            group_send_sem.at[number(piece), n],
            group_recv_sem.at[number(piece), slot],
            (i, group_peer(n)),
        )

    def out_copy(piece):
        strip, left, width = piece
        where = (slice(None), pl.ds(strip * STRIP, STRIP), pl.ds(left, width))
        return pltpu.make_async_copy(result.at[where], out_ref.at[where], out_sem.at[number(piece)])

    def each(count, act, first=0):
        def step(n, carry):
            act(n)
            return carry

        lax.fori_loop(first, count, step, 0)

    def render(piece, n):
        strip, at, width = piece
        left = pl.multiple_of(column_peer(n) * block + at, width)
        colours = march(lambda s: slab[strip, s, :, pl.ds(left, width)], depth, extinct)
        row = lax.broadcasted_iota(jnp.int32, (STRIP, width), 0) + strip * STRIP
        column = lax.broadcasted_iota(jnp.int32, (STRIP, width), 1) + left
        inside = (
            (row >= bounds_ref[0, 0, 0])
            & (row < bounds_ref[0, 0, 1])
            & (column >= bounds_ref[0, 0, 2])
            & (column < bounds_ref[0, 0, 3])
        )
        return [encode(jnp.where(inside, colour, 0.0)) for colour in colours]

    def put(buffer, piece, at, codes):
        strip, left, width = piece
        for channel, code in enumerate(codes):
            buffer[strip, at, channel, :, pl.ds(left, width)] = code

    def render_send(piece, n):
        put(sending, piece, n, render(piece, n))

    def render_keep(piece):
        put(landed, piece, i, render(piece, across_x - 1))

    def render_and_send(piece, n):
        render_send(piece, n)
        column_copy(piece, n, i).start()

    def take(buffer, piece, at):
        strip, left, width = piece
        for channel in range(3):
            images[at, channel, :, :width] = decode(buffer[strip, at, channel, :, pl.ds(left, width)])

    def finish(piece):
        strip, left, width = piece
        take(groups, piece, j)

        def arrive(n):
            peer = group_peer(n)
            group_copy(piece, n, peer).wait_recv()
            take(groups, piece, peer)

        each(across_y, arrive, 1)
        red, green, blue = blend(images, outer_inverse, across_y, width)
        for channel, colour in enumerate((red, green, blue, red + blue)):
            result[channel, pl.ds(strip * STRIP, STRIP), pl.ds(left, width)] = colour
        out_copy(piece).start()

    def drain_column(piece):
        each(across_x - 1, lambda n: column_copy(piece, n, i).wait_send())

    def drain_group(piece):
        each(across_y, lambda n: group_copy(piece, n, j).wait_send(), 1)

    small = [
        pltpu.make_async_copy(inner_hbm, inner_ref, small_sem.at[0]),
        pltpu.make_async_copy(outer_hbm, outer_ref, small_sem.at[1]),
        pltpu.make_async_copy(bounds_hbm, bounds_ref, small_sem.at[2]),
    ]
    small[2].start()
    each(strips, lambda strip: load(strip).start())
    small[0].start()
    small[1].start()

    barrier = pltpu.get_barrier_semaphore()

    def greet_column(n):
        pl.semaphore_signal(barrier, inc=1, device_id=(column_peer(n), j), device_id_type=MESH)

    def greet_group(n):
        pl.semaphore_signal(barrier, inc=1, device_id=(i, group_peer(n)), device_id_type=MESH)

    each(across_x - 1, greet_column)
    each(across_y, greet_group, 1)

    small[2].wait()
    load(0).wait()
    each(FIRST, lambda n: render_send(pieces[0], n))
    pl.semaphore_wait(barrier, across_x - 1 + across_y - 1)
    each(FIRST, lambda n: column_copy(pieces[0], n, i).start())
    each(across_x - 1, lambda n: render_and_send(pieces[0], n), FIRST)
    render_keep(pieces[0])

    def follow(strip):
        piece = (strip, 0, block)
        load(strip).wait()
        each(across_x - 1, lambda n: render_and_send(piece, n))
        render_keep(piece)

    each(last, follow, 1)
    load(last).wait()
    for piece in pieces[last:]:
        each(across_x - 1, lambda n: render_and_send(piece, n))
        render_keep(piece)

    def invert(order_ref, inverse_ref, count):
        def one(rank):
            found = jnp.int32(0)
            for at in range(count):
                found = jnp.where(order_ref[at] == rank, at, found)
            inverse_ref[rank] = found

        each(count, one)

    small[0].wait()
    small[1].wait()
    invert(inner_ref, inner_inverse, across_x)
    invert(outer_ref, outer_inverse, across_y)

    def advance(piece):
        take(landed, piece, i)

        def arrive(n):
            peer = column_peer(n)
            column_copy(piece, n, peer).wait_recv()
            take(landed, piece, peer)

        each(across_x - 1, arrive)
        width = piece[2]
        put(groups, piece, j, [encode(c) for c in blend(images, inner_inverse, across_x, width)])
        each(across_y, lambda n: group_copy(piece, n, j).start(), 1)

    advance(pieces[0])
    for before, piece in zip(pieces[:-1], pieces[1:]):
        advance(piece)
        finish(before)
        drain_column(before)
        drain_group(before)
    drain_column(pieces[-1])
    finish(pieces[-1])
    drain_group(pieces[-1])
    for piece in pieces:
        out_copy(piece).wait()


def on_device(density, inner_order, outer_order, footprints):
    across_x = lax.axis_size("bx")
    across_y = lax.axis_size("by")
    depth, rows, columns = density.shape[2:]
    extinct = 1.5 / (across_x * across_y * depth)
    side = 1
    while side * side < across_y:
        side *= 2
    block = columns // across_x
    strips = rows // STRIP
    pieces = strips - 1 + CUTS
    strip_shape = (3, STRIP, block)
    hbm = pl.BlockSpec(memory_space=pltpu.HBM)
    return pl.pallas_call(
        functools.partial(kernel, (across_x, across_y, side, depth, rows, columns), extinct),
        out_shape=jax.ShapeDtypeStruct((4, rows, block), jnp.float32),
        in_specs=[hbm] * 4,
        out_specs=hbm,
        scratch_shapes=[
            pltpu.VMEM((4, rows, block), jnp.float32),
            pltpu.VMEM((strips, depth, STRIP, columns), jnp.bfloat16),
            pltpu.VMEM((strips, across_x - 1) + strip_shape, jnp.uint16),
            pltpu.VMEM((strips, across_x) + strip_shape, jnp.uint16),
            pltpu.VMEM((strips, across_y) + strip_shape, jnp.uint16),
            pltpu.VMEM((max(across_x, across_y),) + strip_shape, jnp.float32),
            pltpu.SMEM((across_x,), jnp.int32),
            pltpu.SMEM((across_y,), jnp.int32),
            pltpu.SMEM((1, 1, 4), jnp.int32),
            pltpu.SMEM((across_x,), jnp.int32),
            pltpu.SMEM((across_y,), jnp.int32),
            pltpu.SemaphoreType.DMA((3,)),
            pltpu.SemaphoreType.DMA((strips,)),
            pltpu.SemaphoreType.DMA((pieces, across_x)),
            pltpu.SemaphoreType.DMA((pieces, across_x)),
            pltpu.SemaphoreType.DMA((pieces, across_y)),
            pltpu.SemaphoreType.DMA((pieces, across_y)),
            pltpu.SemaphoreType.DMA((pieces,)),
        ],
        compiler_params=pltpu.CompilerParams(
            collective_id=0, has_side_effects=True, vmem_limit_bytes=60 << 20
        ),
    )(inner_order, outer_order, footprints, density)


def solution(mesh):
    in_specs = (P("bx", "by", None, None, None), P(), P(), P("bx", "by", None))
    out_specs = P(None, None, "bx")
    return jax.shard_map(
        on_device, mesh=mesh, in_specs=in_specs, out_specs=out_specs, check_vma=False
    )
```

```python
import functools

import jax
import jax.numpy as jnp
from jax import lax
from jax.experimental import pallas as pl
from jax.experimental.pallas import tpu as pltpu
from jax.sharding import PartitionSpec as P

MESH = pl.DeviceIdType.MESH
LOG2E = 1.4426950408889634
STRIP = 16
CUTS = 2
FIRST = 2
CODE = 65534.0


def encode(value):
    root = lax.rsqrt(lax.rsqrt(jnp.clip(value, 0.0, 1.0)))
    return (root * CODE + 0.5).astype(jnp.int32).astype(jnp.uint16)


def decode(code):
    root = code.astype(jnp.int32).astype(jnp.float32)
    square = root * root * (1.0 / (CODE * CODE))
    return square * square


def march(load, depth, extinct):
    transmit = tanhs = green = None
    for sample in range(depth):
        values = load(sample).astype(jnp.float32)
        square = values * values
        bend = jnp.minimum((2.5 - values) * (2.0 * LOG2E), 0.0)
        survive = jnp.exp2(square * (-extinct * LOG2E) + bend)
        bell = jnp.exp2(square * (-0.5 * LOG2E))
        slope = jnp.tanh(values)
        if sample == 0:
            left = survive
            weight = 1.0 - survive
            tanhs = weight * slope
            green = weight * bell
        else:
            left = transmit * survive
            weight = transmit - left
            tanhs = tanhs + weight * slope
            green = green + weight * bell
        transmit = left
    opaque = 1.0 - transmit
    return 0.5 * (opaque + tanhs), green, 0.5 * (opaque - tanhs)


def blend(images, order_ref, count, width):
    red = green = blue = through = None
    for rank in range(count):
        at = order_ref[rank]
        r, g, b = (images[at, channel, :, :width] for channel in range(3))
        clear = 1.0 - (r + b)
        if rank == 0:
            red, green, blue, through = r, g, b, clear
        else:
            red = red + through * r
            green = green + through * g
            blue = blue + through * b
            through = through * clear
    return red, green, blue


def kernel(
    sizes,
    extinct,
    inner_hbm,
    outer_hbm,
    bounds_hbm,
    density_ref,
    out_ref,
    result,
    slab,
    sending,
    landed,
    groups,
    images,
    inner_ref,
    outer_ref,
    bounds_ref,
    inner_inverse,
    outer_inverse,
    small_sem,
    load_sem,
    send_sem,
    recv_sem,
    group_send_sem,
    group_recv_sem,
    out_sem,
):
    across_x, across_y, side, depth, rows, columns = sizes
    chips = across_x // 2
    block = columns // across_x
    strips = rows // STRIP
    cut = block // CUTS
    last = strips - 1
    pieces = [(strip, 0, block) for strip in range(last)]
    pieces += [(last, cut * at, cut) for at in range(CUTS)]
    i = lax.axis_index("bx")
    j = lax.axis_index("by")
    z, core = lax.div(i, 2), lax.rem(i, 2)
    x, y = lax.div(j, side), lax.rem(j, side)

    def column_peer(n):
        step = n % chips
        hops = chips // 2 + (1 - 2 * (step % 2)) * ((step + 1) // 2)
        return lax.rem(z + hops, chips) * 2 + lax.rem(core + 1 - n // chips, 2)

    def far(k):
        return 2 - k + 3 * (k // 2) - 2 * ((k + 1) // 4)

    def group_peer(n):
        return lax.rem(x + far(n // side), side) * side + lax.rem(y + far(n % side), side)

    def load(strip):
        return pltpu.make_async_copy(
            density_ref.at[0, 0, :, pl.ds(pl.multiple_of(strip * STRIP, STRIP), STRIP), :],
            slab.at[strip],
            load_sem.at[strip],
        )

    def remote(src, dst, sends, recvs, device):
        return pltpu.make_async_remote_copy(
            src_ref=src, dst_ref=dst, send_sem=sends, recv_sem=recvs, device_id=device, device_id_type=MESH
        )

    def view(buffer, piece, at):
        strip, left, width = piece
        return buffer.at[strip, at, :, :, pl.ds(left, width)]

    def number(piece):
        strip, left, width = piece
        return strip + left // width

    def column_copy(piece, n, slot):
        return remote(
            view(sending, piece, n),
            view(landed, piece, slot),
            send_sem.at[number(piece), n],
            recv_sem.at[number(piece), slot],
            (column_peer(n), j),
        )

    def group_copy(piece, n, slot):
        return remote(
            view(groups, piece, j),
            view(groups, piece, slot),
            group_send_sem.at[number(piece), n],
            group_recv_sem.at[number(piece), slot],
            (i, group_peer(n)),
        )

    def out_copy(piece):
        strip, left, width = piece
        where = (slice(None), pl.ds(strip * STRIP, STRIP), pl.ds(left, width))
        return pltpu.make_async_copy(result.at[where], out_ref.at[where], out_sem.at[number(piece)])

    def each(count, act, first=0, flat=False):
        if flat:
            for n in range(first, count):
                act(n)
            return

        def step(n, carry):
            act(n)
            return carry

        lax.fori_loop(first, count, step, 0)

    def render(piece, n):
        strip, at, width = piece
        left = pl.multiple_of(column_peer(n) * block + at, width)
        colours = march(lambda s: slab[strip, s, :, pl.ds(left, width)], depth, extinct)
        row = lax.broadcasted_iota(jnp.int32, (STRIP, width), 0) + strip * STRIP
        column = lax.broadcasted_iota(jnp.int32, (STRIP, width), 1) + left
        inside = (
            (row >= bounds_ref[0, 0, 0])
            & (row < bounds_ref[0, 0, 1])
            & (column >= bounds_ref[0, 0, 2])
            & (column < bounds_ref[0, 0, 3])
        )
        return [encode(jnp.where(inside, colour, 0.0)) for colour in colours]

    def put(buffer, piece, at, codes):
        strip, left, width = piece
        for channel, code in enumerate(codes):
            buffer[strip, at, channel, :, pl.ds(left, width)] = code

    def render_send(piece, n):
        put(sending, piece, n, render(piece, n))

    def render_keep(piece):
        put(landed, piece, i, render(piece, across_x - 1))

    def render_and_send(piece, n):
        render_send(piece, n)
        column_copy(piece, n, i).start()

    def take(buffer, piece, at):
        strip, left, width = piece
        for channel in range(3):
            images[at, channel, :, :width] = decode(buffer[strip, at, channel, :, pl.ds(left, width)])

    def finish(piece):
        strip, left, width = piece
        take(groups, piece, j)

        def arrive(n):
            peer = group_peer(n)
            group_copy(piece, n, peer).wait_recv()
            take(groups, piece, peer)

        each(across_y - 1, arrive, 0, piece is pieces[-1])
        red, green, blue = blend(images, outer_inverse, across_y, width)
        for channel, colour in enumerate((red, green, blue, red + blue)):
            result[channel, pl.ds(strip * STRIP, STRIP), pl.ds(left, width)] = colour
        out_copy(piece).start()

    def drain_column(piece):
        each(across_x - 1, lambda n: column_copy(piece, n, i).wait_send())

    def drain_group(piece):
        each(across_y - 1, lambda n: group_copy(piece, n, j).wait_send(), 0, piece is pieces[-1])

    small = [
        pltpu.make_async_copy(inner_hbm, inner_ref, small_sem.at[0]),
        pltpu.make_async_copy(outer_hbm, outer_ref, small_sem.at[1]),
        pltpu.make_async_copy(bounds_hbm, bounds_ref, small_sem.at[2]),
    ]
    small[2].start()
    load(0).start()

    barrier = pltpu.get_barrier_semaphore()

    def greet_column(n):
        pl.semaphore_signal(barrier, inc=1, device_id=(column_peer(n), j), device_id_type=MESH)

    def greet_group(n):
        pl.semaphore_signal(barrier, inc=1, device_id=(i, group_peer(n)), device_id_type=MESH)

    each(across_x - 1, greet_column, 0, True)
    each(across_y - 1, greet_group, 0, True)

    each(strips, lambda strip: load(strip).start(), 1)
    small[0].start()
    small[1].start()
    small[2].wait()
    load(0).wait()
    each(FIRST, lambda n: render_send(pieces[0], n))
    pl.semaphore_wait(barrier, across_x - 1 + across_y - 1)
    each(FIRST, lambda n: column_copy(pieces[0], n, i).start())
    each(across_x - 1, lambda n: render_and_send(pieces[0], n), FIRST)
    render_keep(pieces[0])

    def follow(strip):
        piece = (strip, 0, block)
        load(strip).wait()
        each(across_x - 1, lambda n: render_and_send(piece, n))
        render_keep(piece)

    each(last, follow, 1)
    load(last).wait()
    for piece in pieces[last:]:
        each(across_x - 1, lambda n: render_and_send(piece, n))
        render_keep(piece)

    def invert(order_ref, inverse_ref, count):
        def one(rank):
            found = jnp.int32(0)
            for at in range(count):
                found = jnp.where(order_ref[at] == rank, at, found)
            inverse_ref[rank] = found

        each(count, one)

    small[0].wait()
    small[1].wait()
    invert(inner_ref, inner_inverse, across_x)
    invert(outer_ref, outer_inverse, across_y)

    def advance(piece):
        take(landed, piece, i)

        def arrive(n):
            peer = column_peer(n)
            column_copy(piece, n, peer).wait_recv()
            take(landed, piece, peer)

        each(across_x - 1, arrive, 0, piece is pieces[-1])
        width = piece[2]
        put(groups, piece, j, [encode(c) for c in blend(images, inner_inverse, across_x, width)])
        each(across_y - 1, lambda n: group_copy(piece, n, j).start(), 0, piece is pieces[-1])

    advance(pieces[0])
    for before, piece in zip(pieces[:-1], pieces[1:]):
        advance(piece)
        finish(before)
        drain_column(before)
        drain_group(before)
    drain_column(pieces[-1])
    finish(pieces[-1])
    drain_group(pieces[-1])
    for piece in pieces:
        out_copy(piece).wait()


def on_device(density, inner_order, outer_order, footprints):
    across_x = lax.axis_size("bx")
    across_y = lax.axis_size("by")
    depth, rows, columns = density.shape[2:]
    extinct = 1.5 / (across_x * across_y * depth)
    side = 1
    while side * side < across_y:
        side *= 2
    block = columns // across_x
    strips = rows // STRIP
    pieces = strips - 1 + CUTS
    strip_shape = (3, STRIP, block)
    hbm = pl.BlockSpec(memory_space=pltpu.HBM)
    return pl.pallas_call(
        functools.partial(kernel, (across_x, across_y, side, depth, rows, columns), extinct),
        out_shape=jax.ShapeDtypeStruct((4, rows, block), jnp.float32),
        in_specs=[hbm] * 4,
        out_specs=hbm,
        scratch_shapes=[
            pltpu.VMEM((4, rows, block), jnp.float32),
            pltpu.VMEM((strips, depth, STRIP, columns), jnp.bfloat16),
            pltpu.VMEM((strips, across_x - 1) + strip_shape, jnp.uint16),
            pltpu.VMEM((strips, across_x) + strip_shape, jnp.uint16),
            pltpu.VMEM((strips, across_y) + strip_shape, jnp.uint16),
            pltpu.VMEM((max(across_x, across_y),) + strip_shape, jnp.float32),
            pltpu.SMEM((across_x,), jnp.int32),
            pltpu.SMEM((across_y,), jnp.int32),
            pltpu.SMEM((1, 1, 4), jnp.int32),
            pltpu.SMEM((across_x,), jnp.int32),
            pltpu.SMEM((across_y,), jnp.int32),
            pltpu.SemaphoreType.DMA((3,)),
            pltpu.SemaphoreType.DMA((strips,)),
            pltpu.SemaphoreType.DMA((pieces, across_x)),
            pltpu.SemaphoreType.DMA((pieces, across_x)),
            pltpu.SemaphoreType.DMA((pieces, across_y)),
            pltpu.SemaphoreType.DMA((pieces, across_y)),
            pltpu.SemaphoreType.DMA((pieces,)),
        ],
        compiler_params=pltpu.CompilerParams(
            collective_id=0, has_side_effects=True, vmem_limit_bytes=60 << 20
        ),
    )(inner_order, outer_order, footprints, density)


def solution(mesh):
    in_specs = (P("bx", "by", None, None, None), P(), P(), P("bx", "by", None))
    out_specs = P(None, None, "bx")
    return jax.shard_map(
        on_device, mesh=mesh, in_specs=in_specs, out_specs=out_specs, check_vma=False
    )
```

```python
import functools

import jax
import jax.numpy as jnp
from jax import lax
from jax.experimental import pallas as pl
from jax.experimental.pallas import tpu as pltpu
from jax.sharding import PartitionSpec as P

MESH = pl.DeviceIdType.MESH
LOG2E = 1.4426950408889634
STRIP = 16
CUTS = 2
FIRST = 2
CODE = 65534.0


def encode(value):
    root = lax.rsqrt(lax.rsqrt(jnp.clip(value, 0.0, 1.0)))
    return (root * CODE + 0.5).astype(jnp.int32).astype(jnp.uint16)


def decode(code):
    root = code.astype(jnp.int32).astype(jnp.float32)
    square = root * root * (1.0 / (CODE * CODE))
    return square * square


def march(load, depth, extinct):
    transmit = tanhs = green = None
    for sample in range(depth):
        values = load(sample).astype(jnp.float32)
        square = values * values
        bend = jnp.minimum((2.5 - values) * (2.0 * LOG2E), 0.0)
        survive = jnp.exp2(square * (-extinct * LOG2E) + bend)
        bell = jnp.exp2(square * (-0.5 * LOG2E))
        slope = jnp.tanh(values)
        if sample == 0:
            left = survive
            weight = 1.0 - survive
            tanhs = weight * slope
            green = weight * bell
        else:
            left = transmit * survive
            weight = transmit - left
            tanhs = tanhs + weight * slope
            green = green + weight * bell
        transmit = left
    opaque = 1.0 - transmit
    return 0.5 * (opaque + tanhs), green, 0.5 * (opaque - tanhs)


def blend(images, order_ref, count, width):
    red = green = blue = through = None
    for rank in range(count):
        at = order_ref[rank]
        r, g, b = (images[at, channel, :, :width] for channel in range(3))
        clear = 1.0 - (r + b)
        if rank == 0:
            red, green, blue, through = r, g, b, clear
        else:
            red = red + through * r
            green = green + through * g
            blue = blue + through * b
            through = through * clear
    return red, green, blue


def kernel(
    sizes,
    extinct,
    small_hbm,
    density_ref,
    out_ref,
    slab,
    sending,
    landed,
    groups,
    images,
    small_ref,
    inner_inverse,
    outer_inverse,
    small_sem,
    load_sem,
    send_sem,
    recv_sem,
    group_send_sem,
    group_recv_sem,
):
    across_x, across_y, side, depth, rows, columns = sizes
    chips = across_x // 2
    block = columns // across_x
    strips = rows // STRIP
    cut = block // CUTS
    last = strips - 1
    pieces = [(strip, 0, block) for strip in range(last)]
    pieces += [(last, cut * at, cut) for at in range(CUTS)]
    i = lax.axis_index("bx")
    j = lax.axis_index("by")
    z, core = lax.div(i, 2), lax.rem(i, 2)
    x, y = lax.div(j, side), lax.rem(j, side)

    def column_peer(n):
        step = n % chips
        hops = chips // 2 + (1 - 2 * (step % 2)) * ((step + 1) // 2)
        return lax.rem(z + hops, chips) * 2 + lax.rem(core + 1 - n // chips, 2)

    def far(k):
        return 2 - k + 3 * (k // 2) - 2 * ((k + 1) // 4)

    def group_peer(n):
        return lax.rem(x + far(n // side), side) * side + lax.rem(y + far(n % side), side)

    def load(strip):
        return pltpu.make_async_copy(
            density_ref.at[0, 0, :, pl.ds(pl.multiple_of(strip * STRIP, STRIP), STRIP), :],
            slab.at[strip],
            load_sem.at[strip],
        )

    def remote(src, dst, sends, recvs, device):
        return pltpu.make_async_remote_copy(
            src_ref=src, dst_ref=dst, send_sem=sends, recv_sem=recvs, device_id=device, device_id_type=MESH
        )

    def view(buffer, piece, at):
        strip, left, width = piece
        return buffer.at[strip, at, :, :, pl.ds(left, width)]

    def number(piece):
        strip, left, width = piece
        return strip + left // width

    def column_copy(piece, n, slot):
        return remote(
            view(sending, piece, n),
            view(landed, piece, slot),
            send_sem.at[number(piece), n],
            recv_sem.at[number(piece), slot],
            (column_peer(n), j),
        )

    def group_copy(piece, n, slot):
        return remote(
            view(groups, piece, j),
            view(groups, piece, slot),
            group_send_sem.at[number(piece), n],
            group_recv_sem.at[number(piece), slot],
            (i, group_peer(n)),
        )

    def each(count, act, first=0, flat=False):
        if flat:
            for n in range(first, count):
                act(n)
            return

        def step(n, carry):
            act(n)
            return carry

        lax.fori_loop(first, count, step, 0)

    def render(piece, n):
        strip, at, width = piece
        left = pl.multiple_of(column_peer(n) * block + at, width)
        colours = march(lambda s: slab[strip, s, :, pl.ds(left, width)], depth, extinct)
        row = lax.broadcasted_iota(jnp.int32, (STRIP, width), 0) + strip * STRIP
        column = lax.broadcasted_iota(jnp.int32, (STRIP, width), 1) + left
        inside = (
            (row >= small_ref[across_x + across_y])
            & (row < small_ref[across_x + across_y + 1])
            & (column >= small_ref[across_x + across_y + 2])
            & (column < small_ref[across_x + across_y + 3])
        )
        return [encode(jnp.where(inside, colour, 0.0)) for colour in colours]

    def put(buffer, piece, at, codes):
        strip, left, width = piece
        for channel, code in enumerate(codes):
            buffer[strip, at, channel, :, pl.ds(left, width)] = code

    def render_send(piece, n):
        put(sending, piece, n, render(piece, n))

    def render_keep(piece):
        put(landed, piece, i, render(piece, across_x - 1))

    def render_and_send(piece, n):
        render_send(piece, n)
        column_copy(piece, n, i).start()

    def take(buffer, piece, at):
        strip, left, width = piece
        for channel in range(3):
            images[at, channel, :, :width] = decode(buffer[strip, at, channel, :, pl.ds(left, width)])

    def finish(piece):
        strip, left, width = piece
        take(groups, piece, j)

        def arrive(n):
            peer = group_peer(n)
            group_copy(piece, n, peer).wait_recv()
            take(groups, piece, peer)

        each(across_y - 1, arrive, 0, piece is pieces[-1])
        red, green, blue = blend(images, outer_inverse, across_y, width)
        for channel, colour in enumerate((red, green, blue, red + blue)):
            out_ref[channel, pl.ds(strip * STRIP, STRIP), pl.ds(left, width)] = colour

    def drain_column(piece):
        each(across_x - 1, lambda n: column_copy(piece, n, i).wait_send())

    def drain_group(piece):
        each(across_y - 1, lambda n: group_copy(piece, n, j).wait_send(), 0, piece is pieces[-1])

    small = [
        pltpu.make_async_copy(small_hbm, small_ref, small_sem.at[0]),
    ]
    small[0].start()
    load(0).start()

    barrier = pltpu.get_barrier_semaphore()

    def greet_column(n):
        pl.semaphore_signal(barrier, inc=1, device_id=(column_peer(n), j), device_id_type=MESH)

    def greet_group(n):
        pl.semaphore_signal(barrier, inc=1, device_id=(i, group_peer(n)), device_id_type=MESH)

    each(across_x - 1, greet_column, 0, True)
    each(across_y - 1, greet_group, 0, True)

    each(strips, lambda strip: load(strip).start(), 1)
    small[0].wait()
    load(0).wait()
    each(FIRST, lambda n: render_send(pieces[0], n))
    pl.semaphore_wait(barrier, across_x - 1 + across_y - 1)
    each(FIRST, lambda n: column_copy(pieces[0], n, i).start())
    each(across_x - 1, lambda n: render_and_send(pieces[0], n), FIRST)
    render_keep(pieces[0])

    def follow(strip):
        piece = (strip, 0, block)
        load(strip).wait()
        each(across_x - 1, lambda n: render_and_send(piece, n))
        render_keep(piece)

    each(last, follow, 1)
    load(last).wait()
    for piece in pieces[last:]:
        each(across_x - 1, lambda n: render_and_send(piece, n))
        render_keep(piece)

    def invert(order_at, inverse_ref, count):
        def one(rank):
            found = jnp.int32(0)
            for at in range(count):
                found = jnp.where(small_ref[order_at + at] == rank, at, found)
            inverse_ref[rank] = found

        each(count, one)

    invert(0, inner_inverse, across_x)
    invert(across_x, outer_inverse, across_y)

    def advance(piece):
        take(landed, piece, i)

        def arrive(n):
            peer = column_peer(n)
            column_copy(piece, n, peer).wait_recv()
            take(landed, piece, peer)

        each(across_x - 1, arrive, 0, piece is pieces[-1])
        width = piece[2]
        put(groups, piece, j, [encode(c) for c in blend(images, inner_inverse, across_x, width)])
        each(across_y - 1, lambda n: group_copy(piece, n, j).start(), 0, piece is pieces[-1])

    advance(pieces[0])
    for before, piece in zip(pieces[:-1], pieces[1:]):
        advance(piece)
        finish(before)
        drain_column(before)
        drain_group(before)
    drain_column(pieces[-1])
    finish(pieces[-1])
    drain_group(pieces[-1])


def on_device(density, inner_order, outer_order, footprints):
    across_x = lax.axis_size("bx")
    across_y = lax.axis_size("by")
    depth, rows, columns = density.shape[2:]
    extinct = 1.5 / (across_x * across_y * depth)
    side = 1
    while side * side < across_y:
        side *= 2
    block = columns // across_x
    strips = rows // STRIP
    pieces = strips - 1 + CUTS
    strip_shape = (3, STRIP, block)
    hbm = pl.BlockSpec(memory_space=pltpu.HBM)
    return pl.pallas_call(
        functools.partial(kernel, (across_x, across_y, side, depth, rows, columns), extinct),
        out_shape=jax.ShapeDtypeStruct((4, rows, block), jnp.float32),
        in_specs=[pl.BlockSpec(memory_space=pl.ANY), hbm],
        out_specs=pl.BlockSpec(memory_space=pltpu.VMEM),
        scratch_shapes=[
            pltpu.VMEM((strips, depth, STRIP, columns), jnp.bfloat16),
            pltpu.VMEM((strips, across_x - 1) + strip_shape, jnp.uint16),
            pltpu.VMEM((strips, across_x) + strip_shape, jnp.uint16),
            pltpu.VMEM((strips, across_y) + strip_shape, jnp.uint16),
            pltpu.VMEM((max(across_x, across_y),) + strip_shape, jnp.float32),
            pltpu.SMEM((across_x + across_y + 4,), jnp.int32),
            pltpu.SMEM((across_x,), jnp.int32),
            pltpu.SMEM((across_y,), jnp.int32),
            pltpu.SemaphoreType.DMA((3,)),
            pltpu.SemaphoreType.DMA((strips,)),
            pltpu.SemaphoreType.DMA((pieces, across_x)),
            pltpu.SemaphoreType.DMA((pieces, across_x)),
            pltpu.SemaphoreType.DMA((pieces, across_y)),
            pltpu.SemaphoreType.DMA((pieces, across_y)),
        ],
        compiler_params=pltpu.CompilerParams(
            collective_id=0, has_side_effects=True, vmem_limit_bytes=50 << 20
        ),
    )(jnp.concatenate([inner_order, outer_order, footprints[0, 0]]), density)


def solution(mesh):
    in_specs = (P("bx", "by", None, None, None), P(), P(), P("bx", "by", None))
    out_specs = P(None, None, "bx")
    return jax.shard_map(
        on_device, mesh=mesh, in_specs=in_specs, out_specs=out_specs, check_vma=False
    )
```

```python
import functools

import jax
import jax.numpy as jnp
from jax import lax
from jax.experimental import pallas as pl
from jax.experimental.pallas import tpu as pltpu
from jax.sharding import PartitionSpec as P

MESH = pl.DeviceIdType.MESH
LOG2E = 1.4426950408889634
STRIP = 16
CUTS = 2
FIRST = 2
CODE = 65534.0


def encode(value):
    root = lax.rsqrt(lax.rsqrt(jnp.clip(value, 0.0, 1.0)))
    return (root * CODE + 0.5).astype(jnp.int32).astype(jnp.uint16)


def decode(code):
    root = code.astype(jnp.int32).astype(jnp.float32)
    square = root * root * (1.0 / (CODE * CODE))
    return square * square


def march(load, depth, extinct):
    transmit = tanhs = green = None
    for sample in range(depth):
        values = load(sample).astype(jnp.float32)
        square = values * values
        bend = jnp.minimum((2.5 - values) * (2.0 * LOG2E), 0.0)
        survive = jnp.exp2(square * (-extinct * LOG2E) + bend)
        bell = jnp.exp2(square * (-0.5 * LOG2E))
        slope = jnp.tanh(values)
        if sample == 0:
            left = survive
            weight = 1.0 - survive
            tanhs = weight * slope
            green = weight * bell
        else:
            left = transmit * survive
            weight = transmit - left
            tanhs = tanhs + weight * slope
            green = green + weight * bell
        transmit = left
    opaque = 1.0 - transmit
    return 0.5 * (opaque + tanhs), green, 0.5 * (opaque - tanhs)


def blend(images, order_ref, count, width):
    red = green = blue = through = None
    for rank in range(count):
        at = order_ref[rank]
        r, g, b = (images[at, channel, :, :width] for channel in range(3))
        clear = 1.0 - (r + b)
        if rank == 0:
            red, green, blue, through = r, g, b, clear
        else:
            red = red + through * r
            green = green + through * g
            blue = blue + through * b
            through = through * clear
    return red, green, blue


def kernel(
    sizes,
    extinct,
    small_hbm,
    density_ref,
    out_ref,
    slab,
    sending,
    landed,
    groups,
    images,
    small_ref,
    inner_inverse,
    outer_inverse,
    small_sem,
    load_sem,
    send_sem,
    recv_sem,
    group_send_sem,
    group_recv_sem,
):
    across_x, across_y, side, depth, rows, columns = sizes
    chips = across_x // 2
    block = columns // across_x
    strips = rows // STRIP
    cut = block // CUTS
    last = strips - 1
    pieces = [(strip, 0, block) for strip in range(last)]
    pieces += [(last, cut * at, cut) for at in range(CUTS)]
    i = lax.axis_index("bx")
    j = lax.axis_index("by")
    z, core = lax.div(i, 2), lax.rem(i, 2)
    x, y = lax.div(j, side), lax.rem(j, side)

    def column_peer(n):
        step = n % chips
        hops = chips // 2 + (1 - 2 * (step % 2)) * ((step + 1) // 2)
        return lax.rem(z + hops, chips) * 2 + lax.rem(core + 1 - n // chips, 2)

    def far(k):
        return 2 - k + 3 * (k // 2) - 2 * ((k + 1) // 4)

    def group_peer(n):
        return lax.rem(x + far(n // side), side) * side + lax.rem(y + far(n % side), side)

    def load(strip):
        return pltpu.make_async_copy(
            density_ref.at[0, 0, :, pl.ds(pl.multiple_of(strip * STRIP, STRIP), STRIP), :],
            slab.at[strip],
            load_sem.at[strip],
        )

    def remote(src, dst, sends, recvs, device):
        return pltpu.make_async_remote_copy(
            src_ref=src, dst_ref=dst, send_sem=sends, recv_sem=recvs, device_id=device, device_id_type=MESH
        )

    def view(buffer, piece, at):
        strip, left, width = piece
        return buffer.at[strip, at, :, :, pl.ds(left, width)]

    def number(piece):
        strip, left, width = piece
        return strip + left // width

    def column_copy(piece, n, slot):
        return remote(
            view(sending, piece, n),
            view(landed, piece, slot),
            send_sem.at[number(piece), n],
            recv_sem.at[number(piece), slot],
            (column_peer(n), j),
        )

    def group_copy(piece, n, slot):
        return remote(
            view(groups, piece, j),
            view(groups, piece, slot),
            group_send_sem.at[number(piece), n],
            group_recv_sem.at[number(piece), slot],
            (i, group_peer(n)),
        )

    def each(count, act, first=0, flat=False):
        if flat:
            for n in range(first, count):
                act(n)
            return

        def step(n, carry):
            act(n)
            return carry

        lax.fori_loop(first, count, step, 0)

    def render(piece, n):
        strip, at, width = piece
        left = pl.multiple_of(column_peer(n) * block + at, width)
        colours = march(lambda s: slab[strip, s, :, pl.ds(left, width)], depth, extinct)
        row = lax.broadcasted_iota(jnp.int32, (STRIP, width), 0) + strip * STRIP
        column = lax.broadcasted_iota(jnp.int32, (STRIP, width), 1) + left
        inside = (
            (row >= small_ref[across_x + across_y])
            & (row < small_ref[across_x + across_y + 1])
            & (column >= small_ref[across_x + across_y + 2])
            & (column < small_ref[across_x + across_y + 3])
        )
        return [encode(jnp.where(inside, colour, 0.0)) for colour in colours]

    def put(buffer, piece, at, codes):
        strip, left, width = piece
        for channel, code in enumerate(codes):
            buffer[strip, at, channel, :, pl.ds(left, width)] = code

    def render_send(piece, n):
        put(sending, piece, n, render(piece, n))

    def render_keep(piece):
        put(landed, piece, i, render(piece, across_x - 1))

    def render_and_send(piece, n):
        render_send(piece, n)
        column_copy(piece, n, i).start()

    def take(buffer, piece, at):
        strip, left, width = piece
        for channel in range(3):
            images[at, channel, :, :width] = decode(buffer[strip, at, channel, :, pl.ds(left, width)])

    def finish(piece):
        strip, left, width = piece
        take(groups, piece, j)

        def arrive(n):
            peer = group_peer(n)
            group_copy(piece, n, peer).wait_recv()
            take(groups, piece, peer)

        each(across_y - 1, arrive, 0, piece is pieces[-1])
        red, green, blue = blend(images, outer_inverse, across_y, width)
        for channel, colour in enumerate((red, green, blue, red + blue)):
            out_ref[channel, pl.ds(strip * STRIP, STRIP), pl.ds(left, width)] = colour

    def drain_column(piece):
        each(across_x - 1, lambda n: column_copy(piece, n, i).wait_send())

    def drain_group(piece):
        each(across_y - 1, lambda n: group_copy(piece, n, j).wait_send(), 0, piece is pieces[-1])

    small = [
        pltpu.make_async_copy(small_hbm, small_ref, small_sem.at[0]),
    ]
    small[0].start()
    load(0).start()

    barrier = pltpu.get_barrier_semaphore()

    def greet_column(n):
        pl.semaphore_signal(barrier, inc=1, device_id=(column_peer(n), j), device_id_type=MESH)

    def greet_group(n):
        pl.semaphore_signal(barrier, inc=1, device_id=(i, group_peer(n)), device_id_type=MESH)

    each(across_x - 1, greet_column, 0, True)
    each(across_y - 1, greet_group, 0, True)

    each(strips, lambda strip: load(strip).start(), 1)
    small[0].wait()
    load(0).wait()
    each(FIRST, lambda n: render_send(pieces[0], n))
    pl.semaphore_wait(barrier, across_x - 1 + across_y - 1)
    each(FIRST, lambda n: column_copy(pieces[0], n, i).start())
    each(across_x - 1, lambda n: render_and_send(pieces[0], n), FIRST)
    render_keep(pieces[0])

    def follow(strip):
        piece = (strip, 0, block)
        load(strip).wait()
        each(across_x - 1, lambda n: render_and_send(piece, n))
        render_keep(piece)

    each(last, follow, 1)
    load(last).wait()
    for piece in pieces[last:]:
        each(across_x - 1, lambda n: render_and_send(piece, n))
        render_keep(piece)

    def invert(order_at, inverse_ref, count):
        def one(rank):
            found = jnp.int32(0)
            for at in range(count):
                found = jnp.where(small_ref[order_at + at] == rank, at, found)
            inverse_ref[rank] = found

        each(count, one)

    invert(0, inner_inverse, across_x)
    invert(across_x, outer_inverse, across_y)

    def advance(piece):
        take(landed, piece, i)

        def arrive(n):
            peer = column_peer(n)
            column_copy(piece, n, peer).wait_recv()
            take(landed, piece, peer)

        each(across_x - 1, arrive, 0, piece is pieces[-1])
        width = piece[2]
        put(groups, piece, j, [encode(c) for c in blend(images, inner_inverse, across_x, width)])
        each(across_y - 1, lambda n: group_copy(piece, n, j).start(), 0, piece is pieces[-1])

    advance(pieces[0])
    for before, piece in zip(pieces[:-1], pieces[1:]):
        advance(piece)
        finish(before)
        drain_column(before)
        drain_group(before)
    drain_column(pieces[-1])
    drain_group(pieces[-1])
    finish(pieces[-1])


def on_device(density, inner_order, outer_order, footprints):
    across_x = lax.axis_size("bx")
    across_y = lax.axis_size("by")
    depth, rows, columns = density.shape[2:]
    extinct = 1.5 / (across_x * across_y * depth)
    side = 1
    while side * side < across_y:
        side *= 2
    block = columns // across_x
    strips = rows // STRIP
    pieces = strips - 1 + CUTS
    strip_shape = (3, STRIP, block)
    hbm = pl.BlockSpec(memory_space=pltpu.HBM)
    return pl.pallas_call(
        functools.partial(kernel, (across_x, across_y, side, depth, rows, columns), extinct),
        out_shape=jax.ShapeDtypeStruct((4, rows, block), jnp.float32),
        in_specs=[pl.BlockSpec(memory_space=pl.ANY), hbm],
        out_specs=pl.BlockSpec(memory_space=pltpu.VMEM),
        scratch_shapes=[
            pltpu.VMEM((strips, depth, STRIP, columns), jnp.bfloat16),
            pltpu.VMEM((strips, across_x - 1) + strip_shape, jnp.uint16),
            pltpu.VMEM((strips, across_x) + strip_shape, jnp.uint16),
            pltpu.VMEM((strips, across_y) + strip_shape, jnp.uint16),
            pltpu.VMEM((max(across_x, across_y),) + strip_shape, jnp.float32),
            pltpu.SMEM((across_x + across_y + 4,), jnp.int32),
            pltpu.SMEM((across_x,), jnp.int32),
            pltpu.SMEM((across_y,), jnp.int32),
            pltpu.SemaphoreType.DMA((3,)),
            pltpu.SemaphoreType.DMA((strips,)),
            pltpu.SemaphoreType.DMA((pieces, across_x)),
            pltpu.SemaphoreType.DMA((pieces, across_x)),
            pltpu.SemaphoreType.DMA((pieces, across_y)),
            pltpu.SemaphoreType.DMA((pieces, across_y)),
        ],
        compiler_params=pltpu.CompilerParams(
            collective_id=0, has_side_effects=True, vmem_limit_bytes=50 << 20
        ),
    )(jnp.concatenate([inner_order, outer_order, footprints[0, 0]]), density)


def solution(mesh):
    in_specs = (P("bx", "by", None, None, None), P(), P(), P("bx", "by", None))
    out_specs = P(None, None, "bx")
    return jax.shard_map(
        on_device, mesh=mesh, in_specs=in_specs, out_specs=out_specs, check_vma=False
    )
```
